32 devices in a mesh: enc: 8 (over y, x, core), abs: 4 (over z).
Axes of the slice: x: 2, y: 2, z: 4, core: 2. Of those that a mesh axis runs over, the one named last changes fastest.
Arguments:
- tiles: bfloat16 [192, 24, 24, 1024], P('enc', None, None, 'abs'), may hold values from -6 to 6
- w_in: bfloat16 [1024, 1024], replicated, may hold values from -0.1875 to 0.1875
- w_out: bfloat16 [1024, 1024], replicated, may hold values from -0.1875 to 0.1875
- se_down: bfloat16 [1024, 256], replicated, may hold values from -0.1875 to 0.1875
- se_up: bfloat16 [256, 1024], replicated, may hold values from -0.375 to 0.375
- kernel: bfloat16 [9, 1024], replicated, may hold values from -2 to 2
- gain: bfloat16 [1024], replicated, may hold values from 0.5 to 1.5
- token_grads: bfloat16 [320, 144, 1024], P(('enc', 'abs')), may hold values from -6 to 6
- tile_counts: int32 [8, 8], replicated, may hold values from 1 to 9, as said below
- sample_owner: int32 [8, 8], replicated, may hold values from 0 to 7, as said below
- sample_rank: int32 [8, 8], replicated, may hold values from 0 to 7, as said below
Outputs:
- visual: bfloat16 [320, 144, 1024], P(('enc', 'abs'))
- tile_grads: bfloat16 [192, 24, 24, 1024], P('enc', None, None, 'abs')
- w_in_grad: float32 [1024, 1024], P(('enc', 'abs'))
- w_out_grad: float32 [1024, 1024], P(('enc', 'abs'))
- se_down_grad: float32 [1024, 256], P(('enc', 'abs'))
- se_up_grad: float32 [256, 1024], P(('enc', 'abs'))
- kernel_grad: float32 [9, 1024], P(None, ('enc', 'abs'))
- gain_grad: float32 [1024], P(('enc', 'abs'))
The draws below stay inside these ranges and needn't reach their ends.
Inputs may be any that keep to these rules, and one draw needn't show every extreme that they name: `tile_counts`: the samples of every encoder group hold 24 tiles together; the samples owned by one abstractor group hold at most 40 tiles together. `sample_owner`: every row names each abstractor group once. `sample_rank`: the 8 samples owned by one abstractor group have distinct ranks.
All inputs are finite; a program needn't handle non-finite values.
Results may differ from the reference program's by a relative error of at most 0.0066.
Values may be sent and summed in bfloat16 or wider, within the bound.
A program may use at most 192 MiB of HBM per device.

```python
import math
import jax
import jax.numpy as jnp
from jax import lax

D = 1024
R = 256
GRID = 24
P_SIZE = 144
TILES_E = 24
TILES = 192
OWN_CAP = 40
SLOTS = 320
N_ENC = 8


def routing_tables(key):
    groups = N_ENC
    half = groups // 2
    keys = jax.random.split(jax.random.fold_in(key, 31), 6)
    spread = jax.random.randint(keys[0], (half // 2,), 0, 5).astype(jnp.int32)
    spread = spread.at[0].set(4)
    heavy_counts = jnp.concatenate([5 + spread, 5 - spread])
    heavy_counts = heavy_counts[jax.random.permutation(keys[1], half)]
    owner_order = jax.random.permutation(keys[2], groups)
    heavy_index = jnp.argsort(owner_order).astype(jnp.int32)
    shifts = (jax.random.permutation(keys[3], groups) % half).astype(jnp.int32)
    owners = jax.vmap(lambda sub: jax.random.permutation(sub, groups))(jax.random.split(keys[4], groups)).astype(jnp.int32)
    place = heavy_index[owners]
    counts = jnp.where(place < half, heavy_counts[(shifts[:, None] + place) % half], 1).astype(jnp.int32)
    orders = jax.vmap(lambda sub: jax.random.permutation(sub, groups))(jax.random.split(keys[5], groups)).astype(jnp.int32)
    ranks = orders[owners, jnp.arange(groups, dtype=jnp.int32)[:, None]].astype(jnp.int32)
    return (counts, owners, ranks)


def draw_tile_counts(key, part):
    return routing_tables(key)[0]


def draw_sample_owner(key, part):
    return routing_tables(key)[1]


def draw_sample_rank(key, part):
    return routing_tables(key)[2]


def levels(rng, dims, pieces, low, top_value):
    level, own = 1.0, jax.random.fold_in(rng, 6)
    for dim, shards_of in pieces:
        heights = jnp.exp(jax.random.uniform(jax.random.fold_in(own, dim), (shards_of,), jnp.float32, low / len(pieces), top_value / len(pieces)))
        level = level * jnp.repeat(heights, dims[dim] // shards_of).reshape([-1 if axis == dim else 1 for axis in range(len(dims))])
    return level


def bell_draw(stream_key, shape, deviation, limit, cuts=(), held_as=jnp.bfloat16):
    drawn = jax.random.normal(stream_key, shape, jnp.float32) * deviation
    if len(cuts) > 0:
        drawn = levels(stream_key, shape, cuts, -0.22, 0.18) * drawn
    return jnp.clip(drawn, min=-limit, max=limit).astype(held_as)


def setup_inputs(seed: int = 0) -> dict:
    key_of = jax.random.split(jax.random.key(seed), 12)
    return {
        "tiles": bell_draw(key_of[0], (TILES, GRID, GRID, D), 1.0, 6.0, ((0, 8), (3, 4))),
        "w_in": bell_draw(key_of[1], (D, D), D ** -0.5, 0.1875),
        "w_out": bell_draw(key_of[2], (D, D), D ** -0.5, 0.1875),
        "se_down": bell_draw(key_of[3], (D, R), D ** -0.5, 0.1875),
        "se_up": bell_draw(key_of[4], (R, D), R ** -0.5, 0.375),
        "kernel": bell_draw(key_of[5], (9, D), 9 ** -0.5, 2.0),
        "gain": jnp.clip(1.0 + 0.1 * jax.random.normal(key_of[6], (D,), jnp.float32), 0.5, 1.5).astype(jnp.bfloat16),
        "token_grads": bell_draw(key_of[7], (SLOTS, P_SIZE, D), 1.0, 6.0, ((0, 32),)),
        "tile_counts": draw_tile_counts(jax.random.fold_in(key_of[11], 71), 0),
        "sample_owner": draw_sample_owner(jax.random.fold_in(key_of[11], 71), 0),
        "sample_rank": draw_sample_rank(jax.random.fold_in(key_of[11], 71), 0),
    }


NORM_EPS = 1e-06

def route_tables(counts, owners, ranks):
    groups = counts.shape[0]
    start = jnp.cumsum(counts, axis=1, dtype=jnp.int32) - counts
    flat_counts = counts.reshape(-1)
    flat_owners = owners.reshape(-1)
    flat_ranks = ranks.reshape(-1)
    ahead = (flat_owners[:, None] == flat_owners[None, :]) & (flat_ranks[None, :] < flat_ranks[:, None])
    offset = lax.optimization_barrier(jnp.sum(jnp.where(ahead, flat_counts[None, :], 0), axis=1, dtype=jnp.int32)).reshape(groups, groups)
    owner_axis = jnp.arange(groups, dtype=jnp.int32)
    filled = lax.optimization_barrier(jnp.sum(jnp.where(flat_owners[None, :] == owner_axis[:, None], flat_counts[None, :], 0), axis=1, dtype=jnp.int32))
    return (start, offset, filled)

def pool_tiles(raw):
    count, grid, channels = (raw.shape[0], raw.shape[1], raw.shape[3])
    side = grid // 2
    wide = raw.astype(jnp.float32).reshape(count, side, 2, side, 2, channels)
    pooled = (lax.optimization_barrier(jnp.sum(wide, axis=(2, 4))) * 0.25).astype(jnp.bfloat16)
    return pooled.reshape(count, side * side, channels)

def spread_back(grads, grid):
    count, cells, channels = grads.shape
    side = grid // 2
    quarter = (grads.astype(jnp.float32) * 0.25).reshape(count, side, 1, side, 1, channels)
    whole = jnp.broadcast_to(quarter, (count, side, 2, side, 2, channels))
    return whole.reshape(count, grid, grid, channels).astype(jnp.bfloat16)

def depthwise(field, taps, side):
    count, cells, channels = field.shape
    plane = field.reshape(count, side, side, channels)
    padded = jnp.pad(plane, ((0, 0), (1, 1), (1, 1), (0, 0)))
    result = jnp.zeros_like(plane)
    for row_tap in range(3):
        for col_tap in range(3):
            result = result + taps[3 * row_tap + col_tap] * padded[:, row_tap:row_tap + side, col_tap:col_tap + side, :]
    return result.reshape(count, cells, channels)

def depthwise_back(back, taps, side):
    count, cells, channels = back.shape
    plane = back.reshape(count, side, side, channels)
    padded = jnp.pad(plane, ((0, 0), (1, 1), (1, 1), (0, 0)))
    result = jnp.zeros_like(plane)
    for row_tap in range(3):
        for col_tap in range(3):
            result = result + taps[3 * row_tap + col_tap] * padded[:, 2 - row_tap:2 - row_tap + side, 2 - col_tap:2 - col_tap + side, :]
    return result.reshape(count, cells, channels)

def kernel_terms(back, activated, side):
    count, cells, channels = back.shape
    plane = back.reshape(count, side, side, channels)
    padded = jnp.pad(activated.reshape(count, side, side, channels), ((0, 0), (1, 1), (1, 1), (0, 0)))
    rows_out = []
    for row_tap in range(3):
        for col_tap in range(3):
            window = padded[:, row_tap:row_tap + side, col_tap:col_tap + side, :]
            rows_out.append(lax.optimization_barrier(jnp.sum(plane * window, axis=(0, 1, 2))))
    return jnp.stack(rows_out, axis=0)

def silu_slope(value):
    sig = jax.nn.sigmoid(value)
    return sig * (1.0 + value * (1.0 - sig))

def block_forward(pooled, w_in, w_out, se_down, se_up, kernel, gain):
    count, cells, width = pooled.shape
    side = math.isqrt(cells)
    wide = pooled.astype(jnp.float32)
    average = lax.optimization_barrier(jnp.mean(wide, axis=-1, keepdims=True))
    centred = wide - average
    variance = lax.optimization_barrier(jnp.mean(centred * centred, axis=-1, keepdims=True))
    inverse = lax.rsqrt(variance + NORM_EPS)
    standard = centred * inverse
    normed = (standard * gain.astype(jnp.float32)).astype(jnp.bfloat16)
    hidden = jnp.dot(normed.reshape(-1, width), w_in, preferred_element_type=jnp.float32).reshape(count, cells, width)
    activated = jax.nn.silu(hidden)
    spatial = depthwise(activated, kernel.astype(jnp.float32), side)
    mixed = jax.nn.silu(spatial)
    squeeze = lax.optimization_barrier(jnp.mean(mixed, axis=1))
    squeeze_pre = jnp.dot(squeeze, se_down.astype(jnp.float32), precision=lax.Precision.HIGHEST)
    squeeze_act = jax.nn.silu(squeeze_pre)
    excite = jax.nn.sigmoid(jnp.dot(squeeze_act, se_up.astype(jnp.float32), precision=lax.Precision.HIGHEST))
    scaled = (mixed * excite[:, None, :]).astype(jnp.bfloat16)
    output = jnp.dot(scaled.reshape(-1, width), w_out, preferred_element_type=jnp.float32).reshape(count, cells, width)
    block = (wide + output).astype(jnp.bfloat16)
    saved = (standard, inverse, normed, hidden, activated, spatial, mixed, squeeze, squeeze_pre, squeeze_act, excite, scaled)
    return (block, saved)

def block_backward(saved, upstream, w_in, w_out, se_down, se_up, kernel, gain):
    standard, inverse, normed, hidden, activated, spatial, mixed, squeeze, squeeze_pre, squeeze_act, excite, scaled = saved
    count, cells, width = upstream.shape
    side = math.isqrt(cells)
    flat_up = upstream.reshape(-1, width)
    w_out_term = jnp.dot(scaled.reshape(-1, width).T, flat_up, preferred_element_type=jnp.float32)
    back_scaled = jnp.dot(flat_up, w_out.T, preferred_element_type=jnp.float32).reshape(count, cells, width)
    back_excite = lax.optimization_barrier(jnp.sum(back_scaled * mixed, axis=1))
    back_pre = back_excite * excite * (1.0 - excite)
    se_up_term = jnp.dot(squeeze_act.T, back_pre, precision=lax.Precision.HIGHEST)
    back_squeeze_act = jnp.dot(back_pre, se_up.astype(jnp.float32).T, precision=lax.Precision.HIGHEST)
    back_squeeze_pre = back_squeeze_act * silu_slope(squeeze_pre)
    se_down_term = jnp.dot(squeeze.T, back_squeeze_pre, precision=lax.Precision.HIGHEST)
    back_squeeze = jnp.dot(back_squeeze_pre, se_down.astype(jnp.float32).T, precision=lax.Precision.HIGHEST)
    back_mixed = back_scaled * excite[:, None, :] + back_squeeze[:, None, :] / cells
    back_spatial = back_mixed * silu_slope(spatial)
    kernel_term = kernel_terms(back_spatial, activated, side)
    back_act = depthwise_back(back_spatial, kernel.astype(jnp.float32), side)
    back_hidden = (back_act * silu_slope(hidden)).astype(jnp.bfloat16)
    flat_hidden = back_hidden.reshape(-1, width)
    w_in_term = jnp.dot(normed.reshape(-1, width).T, flat_hidden, preferred_element_type=jnp.float32)
    back_normed = jnp.dot(flat_hidden, w_in.T, preferred_element_type=jnp.float32).reshape(count, cells, width)
    gain_term = lax.optimization_barrier(jnp.sum(back_normed * standard, axis=(0, 1)))
    back_x = back_normed * gain.astype(jnp.float32)
    centre_term = lax.optimization_barrier(jnp.mean(back_x, axis=-1, keepdims=True))
    along_term = lax.optimization_barrier(jnp.mean(back_x * standard, axis=-1, keepdims=True))
    back_pooled = upstream.astype(jnp.float32) + inverse * (back_x - centre_term - standard * along_term)
    terms = (w_in_term, w_out_term, se_down_term, se_up_term, kernel_term, gain_term)
    return (back_pooled.astype(jnp.bfloat16), terms)

def reference(tiles, w_in, w_out, se_down, se_up, kernel, gain, token_grads, tile_counts, sample_owner, sample_rank):
    groups = N_ENC
    start, offset, filled = route_tables(tile_counts, sample_owner, sample_rank)
    tile_index = jnp.arange(TILES_E, dtype=jnp.int32)
    sample_axis = jnp.arange(groups, dtype=jnp.int32)
    member = lax.optimization_barrier(jnp.sum((start[:, None, :] <= tile_index[None, :, None]).astype(jnp.int32), axis=2, dtype=jnp.int32)) - 1
    pick = member[:, :, None] == sample_axis[None, None, :]
    owner_of = lax.optimization_barrier(jnp.sum(jnp.where(pick, sample_owner[:, None, :], 0), axis=2, dtype=jnp.int32))
    start_of = lax.optimization_barrier(jnp.sum(jnp.where(pick, start[:, None, :], 0), axis=2, dtype=jnp.int32))
    offset_of = lax.optimization_barrier(jnp.sum(jnp.where(pick, offset[:, None, :], 0), axis=2, dtype=jnp.int32))
    slots = (owner_of * OWN_CAP + offset_of + tile_index[None, :] - start_of).astype(jnp.int32)
    raw = tiles.reshape(groups, TILES_E, GRID, GRID, D)
    init = (jnp.zeros((D, D), jnp.float32), jnp.zeros((D, D), jnp.float32), jnp.zeros((D, R), jnp.float32), jnp.zeros((R, D), jnp.float32), jnp.zeros((9, D), jnp.float32), jnp.zeros((D,), jnp.float32))

    def group_step(totals, inputs):
        raw_group, slot_group = inputs
        pooled = pool_tiles(raw_group)
        upstream = jnp.take(token_grads, slot_group, axis=0)
        block, saved = block_forward(pooled, w_in, w_out, se_down, se_up, kernel, gain)
        back_pooled, terms = block_backward(saved, upstream, w_in, w_out, se_down, se_up, kernel, gain)
        totals = jax.tree.map(lambda left, right: left + right, totals, terms)
        return (totals, (block, spread_back(back_pooled, GRID)))
    totals, (blocks, tile_back) = lax.scan(group_step, init, (raw, slots))
    visual = jnp.zeros((SLOTS, P_SIZE, D), jnp.bfloat16).at[slots.reshape(-1)].set(blocks.reshape(-1, P_SIZE, D))
    scale = 1.0 / math.sqrt(N_ENC * TILES_E * P_SIZE)
    return (visual, tile_back.reshape(TILES, GRID, GRID, D), totals[0] * scale, totals[1] * scale, totals[2] * scale, totals[3] * scale, totals[4] * scale, totals[5] * scale)
```

```python
import functools
import math

import jax
import jax.numpy as jnp
from jax import lax
from jax.experimental import pallas as pl
from jax.experimental.pallas import tpu as pltpu
from jax.sharding import PartitionSpec as P

MOST = 9


NORM_EPS = 1e-06


def route_tables(counts, owners, ranks):
    groups = counts.shape[0]
    start = jnp.cumsum(counts, axis=1, dtype=jnp.int32) - counts
    flat_counts = counts.reshape(-1)
    flat_owners = owners.reshape(-1)
    flat_ranks = ranks.reshape(-1)
    ahead = (flat_owners[:, None] == flat_owners[None, :]) & (
        flat_ranks[None, :] < flat_ranks[:, None]
    )
    offset = jnp.sum(jnp.where(ahead, flat_counts[None, :], 0), axis=1, dtype=jnp.int32).reshape(
        groups, groups
    )
    owner_axis = jnp.arange(groups, dtype=jnp.int32)
    filled = jnp.sum(
        jnp.where(flat_owners[None, :] == owner_axis[:, None], flat_counts[None, :], 0),
        axis=1,
        dtype=jnp.int32,
    )
    return (start, offset, filled)


VMEM_BYTES = 50 * 1024 * 1024
LANES = 128


def params():
    return pltpu.CompilerParams(vmem_limit_bytes=VMEM_BYTES)


def pool_kernel(rows_ref, tile_ref, out_ref, half_ref):
    grid, channels = tile_ref.shape[1], tile_ref.shape[3]
    side = grid // 2
    wide = tile_ref[0].astype(jnp.float32).reshape(side, 2, grid, channels)
    half = (wide[:, 0] + wide[:, 1]).reshape(side * grid, channels)
    cells = side * side
    for part in range(channels // LANES):
        lanes = slice(part * LANES, (part + 1) * LANES)
        half_ref[part] = half[:, lanes]
        even = half_ref[part, pl.ds(0, cells, stride=2), :]
        odd = half_ref[part, pl.ds(1, cells, stride=2), :]
        out_ref[0, :, lanes] = ((even + odd) * 0.25).astype(jnp.bfloat16)


def pool_and_pick(tiles, rows):
    count, grid, _, channels = tiles.shape
    cells = (grid // 2) ** 2
    sends = rows.shape[0]
    return pl.pallas_call(
        pool_kernel,
        out_shape=jax.ShapeDtypeStruct((sends, cells, channels), jnp.bfloat16),
        grid_spec=pltpu.PrefetchScalarGridSpec(
            num_scalar_prefetch=1,
            grid=(sends,),
            in_specs=[
                pl.BlockSpec((1, grid, grid, channels), lambda g, rows: (rows[g], 0, 0, 0))
            ],
            out_specs=pl.BlockSpec((1, cells, channels), lambda g, rows: (g, 0, 0)),
            scratch_shapes=[pltpu.VMEM((channels // LANES, 2 * cells, LANES), jnp.float32)],
        ),
        compiler_params=params(),
        name="pool_and_pick",
    )(rows, tiles)


def spread_kernel(rows_ref, grads_ref, out_ref, half_ref):
    grid, channels = out_ref.shape[1], out_ref.shape[3]
    side = grid // 2
    cells = side * side
    for part in range(channels // LANES):
        lanes = slice(part * LANES, (part + 1) * LANES)
        quarter = grads_ref[0, :, lanes].astype(jnp.float32) * 0.25
        half_ref[part, pl.ds(0, cells, stride=2), :] = quarter
        half_ref[part, pl.ds(1, cells, stride=2), :] = quarter
        half = half_ref[part].reshape(side, 1, grid, LANES)
        whole = jnp.broadcast_to(half, (side, 2, grid, LANES)).reshape(grid, grid, LANES)
        out_ref[0, :, :, lanes] = whole.astype(jnp.bfloat16)


def pick_and_spread(grads, rows, grid):
    _, cells, channels = grads.shape
    count = rows.shape[0]
    return pl.pallas_call(
        spread_kernel,
        out_shape=jax.ShapeDtypeStruct((count, grid, grid, channels), jnp.bfloat16),
        grid_spec=pltpu.PrefetchScalarGridSpec(
            num_scalar_prefetch=1,
            grid=(count,),
            in_specs=[pl.BlockSpec((1, cells, channels), lambda g, rows: (rows[g], 0, 0))],
            out_specs=pl.BlockSpec((1, grid, grid, channels), lambda g, rows: (g, 0, 0, 0)),
            scratch_shapes=[pltpu.VMEM((channels // LANES, 2 * cells, LANES), jnp.float32)],
        ),
        compiler_params=params(),
        name="pick_and_spread",
    )(rows, grads)


def copy_kernel(rows_ref, source_ref, out_ref, sems):
    count = out_ref.shape[0]

    def one(g):
        return pltpu.make_async_copy(source_ref.at[rows_ref[g]], out_ref.at[g], sems.at[g])

    @pl.loop(0, count)
    def _(g):
        one(g).start()

    @pl.loop(0, count)
    def _(g):
        one(g).wait()


def pick_rows(source, rows):
    count = rows.shape[0]
    return pl.pallas_call(
        copy_kernel,
        out_shape=jax.ShapeDtypeStruct((count,) + source.shape[1:], source.dtype),
        grid_spec=pltpu.PrefetchScalarGridSpec(
            num_scalar_prefetch=1,
            grid=(),
            in_specs=[pl.BlockSpec(memory_space=pl.ANY)],
            out_specs=pl.BlockSpec(memory_space=pl.ANY),
            scratch_shapes=[pltpu.SemaphoreType.DMA((count,))],
        ),
        compiler_params=params(),
        name="pick_rows",
    )(rows, source)


def edge_masks(cells, side):
    row = lax.broadcasted_iota(jnp.int32, (cells, LANES), 0)
    col = lax.rem(row, side)
    one = lambda keep: keep.astype(jnp.float32)
    return (
        one(row >= side),
        one(row < cells - side),
        one(col >= 1),
        one(col < side - 1),
    )


def row_neighbours(field, masks, side):
    cells = field.shape[0]
    above = pltpu.roll(field, side, 0) * masks[0]
    below = pltpu.roll(field, cells - side, 0) * masks[1]
    return (above, below)


def col_previous(field, masks):
    return pltpu.roll(field, 1, 0) * masks[2]


def col_next(field, masks):
    return pltpu.roll(field, field.shape[0] - 1, 0) * masks[3]


ROWS = 48


def forward_kernel(
    live_ref, owned_ref, back_ref, w_in_ref, kernel_ref, gain_ref,
    pooled_ref, normed_ref, hidden_ref, spatial_ref, squeeze_ref, excite_ref,
):
    columns, batch, cells, narrow = owned_ref.shape
    width = columns * narrow
    side = math.isqrt(cells)
    first = pl.program_id(0) * batch
    gain = gain_ref[...].astype(jnp.float32)
    for b in range(batch):
        keep = live_ref[first + b] > 0
        for r in range(0, cells, ROWS):
            rows = slice(r, r + ROWS)
            pieces = [owned_ref[c, b, rows, :] for c in range(columns)]
            pooled = jnp.concatenate(pieces, axis=-1)
            wide = jnp.where(keep, pooled.astype(jnp.float32), 0.0)
            pooled_ref[b, rows, :] = wide.astype(jnp.bfloat16)
            average = jnp.mean(wide, axis=-1, keepdims=True)
            centred = wide - average
            variance = jnp.mean(centred * centred, axis=-1, keepdims=True)
            standard = centred * lax.rsqrt(variance + NORM_EPS)
            normed_ref[b, rows, :] = (standard * gain).astype(jnp.bfloat16)
    hidden = jnp.dot(
        normed_ref[...].reshape(batch * cells, width),
        w_in_ref[...],
        preferred_element_type=jnp.float32,
    )
    hidden_ref[...] = hidden.reshape(batch, cells, width)
    masks = edge_masks(cells, side)
    for b in range(batch):

        @pl.loop(0, width // LANES)
        def _(part):
            lanes = pl.ds(pl.multiple_of(part * LANES, LANES), LANES)
            value = hidden_ref[b, :, lanes]
            act = value * jax.nn.sigmoid(value)
            above, below = row_neighbours(act, masks, side)
            taps = kernel_ref[:, lanes]
            spread = [
                taps[c : c + 1] * above + taps[3 + c : 4 + c] * act + taps[6 + c : 7 + c] * below
                for c in range(3)
            ]
            spatial = spread[1] + col_previous(spread[0], masks) + col_next(spread[2], masks)
            spatial_ref[b, :, lanes] = spatial
            mixed = spatial * jax.nn.sigmoid(spatial)
            squeeze_ref[b, :, lanes] = jnp.sum(mixed, axis=0, keepdims=True) * (1.0 / cells)
            excite_ref[b, :, lanes] = jnp.sum(
                back_ref[b, :, lanes] * mixed, axis=0, keepdims=True
            )


def forward_call(owned, back_scaled, live, w_in, taps, gain):
    columns, count, cells, narrow = owned.shape
    width = columns * narrow
    batch = 2 if count % 2 == 0 else 1
    block = lambda: pl.BlockSpec((batch, cells, width), lambda g, live: (g, 0, 0))
    row = lambda: pl.BlockSpec((batch, 1, width), lambda g, live: (g, 0, 0))
    whole = lambda a: pl.BlockSpec(a.shape, lambda g, live: (0,) * a.ndim)
    wide = lambda kind: jax.ShapeDtypeStruct((count, cells, width), kind)
    line = jax.ShapeDtypeStruct((count, 1, width), jnp.float32)
    return pl.pallas_call(
        forward_kernel,
        out_shape=(
            wide(jnp.bfloat16), wide(jnp.bfloat16), wide(jnp.float32), wide(jnp.float32), line, line,
        ),
        grid_spec=pltpu.PrefetchScalarGridSpec(
            num_scalar_prefetch=1,
            grid=(count // batch,),
            in_specs=[
                pl.BlockSpec((columns, batch, cells, narrow), lambda g, live: (0, g, 0, 0)),
                block(), whole(w_in), whole(taps), whole(gain),
            ],
            out_specs=[block(), block(), block(), block(), row(), row()],
        ),
        compiler_params=params(),
        cost_estimate=pl.CostEstimate(
            flops=2 * count * cells * width * width,
            bytes_accessed=30 * count * cells * width,
            transcendentals=4 * count * cells * width,
        ),
        name="forward",
    )(live, owned, back_scaled, w_in, taps, gain)


def backward_kernel(
    pooled_ref, hidden_ref, spatial_ref, back_ref, up_ref, excite_ref, shift_ref,
    w_in_t_ref, kernel_ref, gain_ref,
    back_hidden_ref, back_in_ref, taps_ref, gain_grad_ref, normed_ref,
):
    columns, batch, cells, narrow = back_in_ref.shape
    width = columns * narrow
    side = math.isqrt(cells)

    @pl.when(pl.program_id(0) == 0)
    def _():
        taps_ref[...] = jnp.zeros_like(taps_ref)
        gain_grad_ref[...] = jnp.zeros_like(gain_grad_ref)

    masks = edge_masks(cells, side)
    for b in range(batch):

        @pl.loop(0, width // LANES)
        def _(part):
            lanes = pl.ds(pl.multiple_of(part * LANES, LANES), LANES)
            taps = kernel_ref[:, lanes]
            spatial = spatial_ref[b, :, lanes]
            sig = jax.nn.sigmoid(spatial)
            back_mixed = back_ref[b, :, lanes] * excite_ref[b, :, lanes] + shift_ref[b, :, lanes]
            back = back_mixed * (sig * (1.0 + spatial * (1.0 - sig)))
            above, below = row_neighbours(back, masks, side)
            spread = [
                taps[c : c + 1] * below + taps[3 + c : 4 + c] * back + taps[6 + c : 7 + c] * above
                for c in range(3)
            ]
            back_act = spread[1] + col_next(spread[0], masks) + col_previous(spread[2], masks)
            value = hidden_ref[b, :, lanes]
            sig = jax.nn.sigmoid(value)
            back_hidden_ref[b, :, lanes] = (
                back_act * (sig * (1.0 + value * (1.0 - sig)))
            ).astype(jnp.bfloat16)
            act = value * sig
            above, below = row_neighbours(act, masks, side)
            sides = (
                pltpu.roll(back * masks[2], cells - 1, 0),
                back,
                pltpu.roll(back * masks[3], 1, 0),
            )
            for a, field in enumerate((above, act, below)):
                for c in range(3):
                    tap = 3 * a + c
                    taps_ref[tap : tap + 1, lanes] += jnp.sum(
                        sides[c] * field, axis=0, keepdims=True
                    )

    normed_ref[...] = jnp.dot(
        back_hidden_ref[...].reshape(batch * cells, width),
        w_in_t_ref[...],
        preferred_element_type=jnp.float32,
    )
    gain = gain_ref[...].astype(jnp.float32)
    for b in range(batch):
        for r in range(0, cells, ROWS):
            rows = slice(r, r + ROWS)
            wide = pooled_ref[b, rows, :].astype(jnp.float32)
            average = jnp.mean(wide, axis=-1, keepdims=True)
            centred = wide - average
            variance = jnp.mean(centred * centred, axis=-1, keepdims=True)
            inverse = lax.rsqrt(variance + NORM_EPS)
            standard = centred * inverse
            back_normed = normed_ref[b * cells + r : b * cells + r + ROWS, :]
            gain_grad_ref[...] += jnp.sum(back_normed * standard, axis=0, keepdims=True)
            back_x = back_normed * gain
            centre = jnp.mean(back_x, axis=-1, keepdims=True)
            along = jnp.mean(back_x * standard, axis=-1, keepdims=True)
            result = up_ref[b, rows, :].astype(jnp.float32) + inverse * (
                back_x - centre - standard * along
            )
            result = result.astype(jnp.bfloat16)
            for c in range(columns):
                back_in_ref[c, b, rows, :] = result[:, c * narrow : (c + 1) * narrow]


def backward_call(
    pooled, hidden, spatial, back_scaled, upstream, excite, shift, w_in_t, taps, gain, columns
):
    count, cells, width = pooled.shape
    narrow = width // columns
    batch = 2 if count % 2 == 0 else 1
    block = lambda: pl.BlockSpec((batch, cells, width), lambda g: (g, 0, 0))
    row = lambda: pl.BlockSpec((batch, 1, width), lambda g: (g, 0, 0))
    whole = lambda shape: pl.BlockSpec(shape, lambda g: (0,) * len(shape))
    return pl.pallas_call(
        backward_kernel,
        out_shape=(
            jax.ShapeDtypeStruct((count, cells, width), jnp.bfloat16),
            jax.ShapeDtypeStruct((columns, count, cells, narrow), jnp.bfloat16),
            jax.ShapeDtypeStruct((9, width), jnp.float32),
            jax.ShapeDtypeStruct((1, width), jnp.float32),
        ),
        grid=(count // batch,),
        in_specs=[
            block(), block(), block(), block(), block(), row(), row(),
            whole(w_in_t.shape), whole(taps.shape), whole(gain.shape),
        ],
        out_specs=[
            block(),
            pl.BlockSpec((columns, batch, cells, narrow), lambda g: (0, g, 0, 0)),
            whole((9, width)),
            whole((1, width)),
        ],
        scratch_shapes=[pltpu.VMEM((batch * cells, width), jnp.float32)],
        compiler_params=params(),
        cost_estimate=pl.CostEstimate(
            flops=2 * count * cells * width * width,
            bytes_accessed=30 * count * cells * width,
            transcendentals=4 * count * cells * width,
        ),
        name="backward",
    )(pooled, hidden, spatial, back_scaled, upstream, excite, shift, w_in_t, taps, gain)


def silu_slope(value):
    sig = jax.nn.sigmoid(value)
    return sig * (1.0 + value * (1.0 - sig))


def pick_row(table, chosen):
    return jnp.sum(jnp.where(chosen[:, None], table, 0), axis=0, dtype=jnp.int32)


def share_out(terms, groups, columns):
    rows = [term.shape[1] for term in terms]
    packed = jnp.concatenate([term.astype(jnp.bfloat16) for term in terms], axis=1)
    packed = packed.reshape((groups, columns) + packed.shape[1:])
    arrived = lax.all_to_all(packed, "enc", split_axis=0, concat_axis=0, tiled=True)
    partial = jnp.sum(arrived.astype(jnp.float32), axis=0).astype(jnp.bfloat16)
    arrived = lax.all_to_all(partial, "abs", split_axis=0, concat_axis=0, tiled=True)
    total = jnp.sum(arrived.astype(jnp.float32), axis=0)
    shares, at = [], 0
    for count in rows:
        shares.append(total[at : at + count])
        at += count
    return shares


def local(
    tiles,
    w_in,
    w_out,
    se_down,
    se_up,
    kernel,
    gain,
    token_grads,
    tile_counts,
    sample_owner,
    sample_rank,
):
    groups = lax.axis_size("enc")
    columns = lax.axis_size("abs")
    group_id = lax.axis_index("enc")
    column_id = lax.axis_index("abs")
    local_tiles = tiles.shape[0]
    owned_rows = token_grads.shape[0]
    capacity = owned_rows * columns
    cells = token_grads.shape[1]
    start, offset, filled = route_tables(tile_counts, sample_owner, sample_rank)
    sources = jnp.arange(groups, dtype=jnp.int32)
    slot_steps = jnp.arange(MOST, dtype=jnp.int32)
    this_group = sources == group_id
    owner_row = pick_row(sample_owner, this_group)
    count_row = pick_row(tile_counts, this_group)
    start_row = pick_row(start, this_group)
    chosen = owner_row[None, :] == sources[:, None]
    send_count = jnp.sum(jnp.where(chosen, count_row[None, :], 0), axis=1, dtype=jnp.int32)
    send_start = jnp.sum(jnp.where(chosen, start_row[None, :], 0), axis=1, dtype=jnp.int32)
    send_rows = (
        send_start[:, None] + jnp.minimum(slot_steps[None, :], send_count[:, None] - 1)
    ).reshape(-1)
    arriving = sample_owner == group_id
    recv_count = jnp.sum(jnp.where(arriving, tile_counts, 0), axis=1, dtype=jnp.int32)
    recv_offset = jnp.sum(jnp.where(arriving, offset, 0), axis=1, dtype=jnp.int32)
    positions = jnp.arange(capacity, dtype=jnp.int32)
    inside = (positions[:, None] >= recv_offset[None, :]) & (
        positions[:, None] < (recv_offset + recv_count)[None, :]
    )
    gather_rows = jnp.sum(
        jnp.where(inside, sources[None, :] * MOST + positions[:, None] - recv_offset[None, :], 0),
        axis=1,
        dtype=jnp.int32,
    )
    return_rows = (
        recv_offset[:, None] + jnp.minimum(slot_steps[None, :], recv_count[:, None] - 1)
    ).reshape(-1)
    tile_ids = jnp.arange(local_tiles, dtype=jnp.int32)
    member = (
        jnp.sum(
            (start_row[None, :] <= tile_ids[:, None]).astype(jnp.int32), axis=1, dtype=jnp.int32
        )
        - 1
    )
    which = member[:, None] == sources[None, :]
    member_owner = jnp.sum(jnp.where(which, owner_row[None, :], 0), axis=1, dtype=jnp.int32)
    member_start = jnp.sum(jnp.where(which, start_row[None, :], 0), axis=1, dtype=jnp.int32)
    unpack_rows = member_owner * MOST + tile_ids - member_start
    filled_here = jnp.sum(jnp.where(this_group, filled, 0), dtype=jnp.int32)
    live = column_id * owned_rows + jnp.arange(owned_rows, dtype=jnp.int32) < filled_here
    width = token_grads.shape[2]
    narrow = tiles.shape[3]
    devices = groups * columns
    flat = (owned_rows * cells, width)
    upstream = jnp.where(live[:, None, None], token_grads, jnp.zeros_like(token_grads))
    back_scaled = jnp.dot(
        upstream.reshape(flat), w_out.T, preferred_element_type=jnp.float32
    ).reshape(upstream.shape)
    taps = kernel.astype(jnp.float32)
    gain_row = gain.reshape(1, width)

    send = pool_and_pick(tiles, send_rows).reshape(groups, MOST, cells, narrow)
    received = lax.all_to_all(send, "enc", split_axis=0, concat_axis=0, tiled=True)
    compact = pick_rows(received.reshape(groups * MOST, cells, narrow), gather_rows)
    owned = lax.all_to_all(
        compact.reshape(columns, owned_rows, cells, narrow),
        "abs",
        split_axis=0,
        concat_axis=0,
        tiled=True,
    )
    pooled, normed, hidden, spatial, squeeze, back_excite = forward_call(
        owned, back_scaled, live.astype(jnp.int32), w_in, taps, gain_row
    )

    exact = functools.partial(jnp.dot, precision=lax.Precision.HIGHEST)
    squeeze = squeeze.reshape(owned_rows, width)
    down, up = se_down.astype(jnp.float32), se_up.astype(jnp.float32)
    squeeze_pre = exact(squeeze, down)
    squeeze_act = jax.nn.silu(squeeze_pre)
    excite = jax.nn.sigmoid(exact(squeeze_act, up))
    back_pre = back_excite.reshape(owned_rows, width) * excite * (1.0 - excite)
    back_squeeze_pre = exact(back_pre, up.T) * silu_slope(squeeze_pre)
    shift = exact(back_squeeze_pre, down.T) / cells

    back_hidden, back_in, taps_term, gain_term = backward_call(
        pooled, hidden, spatial, back_scaled, upstream,
        excite[:, None, :], shift[:, None, :], w_in.T, taps, gain_row, columns,
    )
    back_narrow = lax.all_to_all(back_in, "abs", split_axis=0, concat_axis=0, tiled=True)
    returned = pick_rows(back_narrow.reshape(capacity, cells, narrow), return_rows)
    arrived = lax.all_to_all(
        returned.reshape(groups, MOST, cells, narrow), "enc", split_axis=0, concat_axis=0, tiled=True
    )
    tile_grads = pick_and_spread(
        arrived.reshape(groups * MOST, cells, narrow), unpack_rows, tiles.shape[1]
    )

    scaled = (jax.nn.silu(spatial) * excite[:, None, :]).astype(jnp.bfloat16)
    output = jnp.dot(scaled.reshape(flat), w_out, preferred_element_type=jnp.float32)
    visual = (pooled.astype(jnp.float32) + output.reshape(pooled.shape)).astype(jnp.bfloat16)

    w_out_term = jnp.dot(
        scaled.reshape(flat).T, upstream.reshape(flat), preferred_element_type=jnp.float32
    )
    w_in_term = jnp.dot(
        normed.reshape(flat).T, back_hidden.reshape(flat), preferred_element_type=jnp.float32
    )
    se_up_term = exact(squeeze_act.T, back_pre)
    se_down_term = exact(squeeze.T, back_squeeze_pre)
    share = width // devices
    small = jnp.concatenate(
        [
            taps_term.reshape(9, devices, share).transpose(1, 0, 2).reshape(devices, 9 * share),
            gain_term.reshape(devices, share),
        ],
        axis=1,
    )
    lines = -(-10 * share // width)
    small = jnp.pad(small, ((0, 0), (0, lines * width - 10 * share)))
    dest = lambda term: term.reshape(devices, -1, width)
    early = share_out([dest(w_out_term), dest(se_down_term), dest(se_up_term)], groups, columns)
    late = share_out([dest(w_in_term), dest(small)], groups, columns)
    scale = 1.0 / math.sqrt(groups * local_tiles * cells)
    lasts = late[1].reshape(-1)
    return (
        visual,
        tile_grads,
        late[0] * scale,
        early[0] * scale,
        early[1].reshape(-1, se_down.shape[1]) * scale,
        early[2] * scale,
        lasts[: 9 * share].reshape(9, share) * scale,
        lasts[9 * share : 10 * share] * scale,
    )


def solution(mesh):
    return jax.shard_map(
        local,
        mesh=mesh,
        in_specs=(
            P("enc", None, None, "abs"),
            P(),
            P(),
            P(),
            P(),
            P(),
            P(),
            P(("enc", "abs"), None, None),
            P(),
            P(),
            P(),
        ),
        out_specs=(
            P(("enc", "abs"), None, None),
            P("enc", None, None, "abs"),
            P(("enc", "abs"), None),
            P(("enc", "abs"), None),
            P(("enc", "abs"), None),
            P(("enc", "abs"), None),
            P(None, ("enc", "abs")),
            P(("enc", "abs")),
        ),
        check_vma=False,
    )
```

```python
import functools
import math

import jax
import jax.numpy as jnp
from jax import lax
from jax.experimental import pallas as pl
from jax.experimental.pallas import tpu as pltpu
from jax.sharding import PartitionSpec as P

MOST = 9


NORM_EPS = 1e-06


def route_tables(counts, owners, ranks):
    groups = counts.shape[0]
    start = jnp.cumsum(counts, axis=1, dtype=jnp.int32) - counts
    flat_counts = counts.reshape(-1)
    flat_owners = owners.reshape(-1)
    flat_ranks = ranks.reshape(-1)
    ahead = (flat_owners[:, None] == flat_owners[None, :]) & (
        flat_ranks[None, :] < flat_ranks[:, None]
    )
    offset = jnp.sum(jnp.where(ahead, flat_counts[None, :], 0), axis=1, dtype=jnp.int32).reshape(
        groups, groups
    )
    owner_axis = jnp.arange(groups, dtype=jnp.int32)
    filled = jnp.sum(
        jnp.where(flat_owners[None, :] == owner_axis[:, None], flat_counts[None, :], 0),
        axis=1,
        dtype=jnp.int32,
    )
    return (start, offset, filled)


VMEM_BYTES = 50 * 1024 * 1024
LANES = 128


def params():
    return pltpu.CompilerParams(vmem_limit_bytes=VMEM_BYTES)


def pool_kernel(rows_ref, tile_ref, out_ref, half_ref):
    grid, channels = tile_ref.shape[1], tile_ref.shape[3]
    side = grid // 2
    wide = tile_ref[0].astype(jnp.float32).reshape(side, 2, grid, channels)
    half = (wide[:, 0] + wide[:, 1]).reshape(side * grid, channels)
    cells = side * side
    for part in range(channels // LANES):
        lanes = slice(part * LANES, (part + 1) * LANES)
        half_ref[part] = half[:, lanes]
        even = half_ref[part, pl.ds(0, cells, stride=2), :]
        odd = half_ref[part, pl.ds(1, cells, stride=2), :]
        out_ref[0, :, lanes] = ((even + odd) * 0.25).astype(jnp.bfloat16)


def pool_and_place(tiles, rows, sends):
    count, grid, _, channels = tiles.shape
    cells = (grid // 2) ** 2
    return pl.pallas_call(
        pool_kernel,
        out_shape=jax.ShapeDtypeStruct((sends, cells, channels), jnp.bfloat16),
        grid_spec=pltpu.PrefetchScalarGridSpec(
            num_scalar_prefetch=1,
            grid=(count,),
            in_specs=[pl.BlockSpec((1, grid, grid, channels), lambda g, rows: (g, 0, 0, 0))],
            out_specs=pl.BlockSpec((1, cells, channels), lambda g, rows: (rows[g], 0, 0)),
            scratch_shapes=[pltpu.VMEM((channels // LANES, 2 * cells, LANES), jnp.float32)],
        ),
        compiler_params=params(),
        name="pool_and_place",
    )(rows, tiles)


def spread_kernel(rows_ref, grads_ref, out_ref, half_ref):
    grid, channels = out_ref.shape[1], out_ref.shape[3]
    side = grid // 2
    cells = side * side
    for part in range(channels // LANES):
        lanes = slice(part * LANES, (part + 1) * LANES)
        quarter = grads_ref[0, :, lanes].astype(jnp.float32) * 0.25
        half_ref[part, pl.ds(0, cells, stride=2), :] = quarter
        half_ref[part, pl.ds(1, cells, stride=2), :] = quarter
        half = half_ref[part].reshape(side, 1, grid, LANES)
        whole = jnp.broadcast_to(half, (side, 2, grid, LANES)).reshape(grid, grid, LANES)
        out_ref[0, :, :, lanes] = whole.astype(jnp.bfloat16)


def pick_and_spread(grads, rows, grid):
    _, cells, channels = grads.shape
    count = rows.shape[0]
    return pl.pallas_call(
        spread_kernel,
        out_shape=jax.ShapeDtypeStruct((count, grid, grid, channels), jnp.bfloat16),
        grid_spec=pltpu.PrefetchScalarGridSpec(
            num_scalar_prefetch=1,
            grid=(count,),
            in_specs=[pl.BlockSpec((1, cells, channels), lambda g, rows: (rows[g], 0, 0))],
            out_specs=pl.BlockSpec((1, grid, grid, channels), lambda g, rows: (g, 0, 0, 0)),
            scratch_shapes=[pltpu.VMEM((channels // LANES, 2 * cells, LANES), jnp.float32)],
        ),
        compiler_params=params(),
        name="pick_and_spread",
    )(rows, grads)


def copy_kernel(rows_ref, source_ref, out_ref, sems):
    count = out_ref.shape[0]

    def one(g):
        return pltpu.make_async_copy(source_ref.at[rows_ref[g]], out_ref.at[g], sems.at[g])

    @pl.loop(0, count)
    def _(g):
        one(g).start()

    @pl.loop(0, count)
    def _(g):
        one(g).wait()


def pick_rows(source, rows):
    count = rows.shape[0]
    return pl.pallas_call(
        copy_kernel,
        out_shape=jax.ShapeDtypeStruct((count,) + source.shape[1:], source.dtype),
        grid_spec=pltpu.PrefetchScalarGridSpec(
            num_scalar_prefetch=1,
            grid=(),
            in_specs=[pl.BlockSpec(memory_space=pl.ANY)],
            out_specs=pl.BlockSpec(memory_space=pltpu.VMEM),
            scratch_shapes=[pltpu.SemaphoreType.DMA((count,))],
        ),
        compiler_params=params(),
        name="pick_rows",
    )(rows, source)


def place_kernel(rows_ref, live_ref, source_ref, out_ref, sems):
    count = source_ref.shape[0]

    def one(g):
        return pltpu.make_async_copy(source_ref.at[g], out_ref.at[rows_ref[g]], sems.at[g])

    @pl.loop(0, count)
    def _(g):
        @pl.when(live_ref[g] > 0)
        def _():
            one(g).start()

    @pl.loop(0, count)
    def _(g):
        @pl.when(live_ref[g] > 0)
        def _():
            one(g).wait()


def place_rows(source, rows, live, sends):
    count = rows.shape[0]
    return pl.pallas_call(
        place_kernel,
        out_shape=jax.ShapeDtypeStruct((sends,) + source.shape[1:], source.dtype),
        grid_spec=pltpu.PrefetchScalarGridSpec(
            num_scalar_prefetch=2,
            grid=(),
            in_specs=[pl.BlockSpec(memory_space=pltpu.VMEM)],
            out_specs=pl.BlockSpec(memory_space=pl.ANY),
            scratch_shapes=[pltpu.SemaphoreType.DMA((count,))],
        ),
        compiler_params=params(),
        name="place_rows",
    )(rows, live, source)


def exchange_kernel(axes, sizes, *refs):
    jobs = len(axes)
    sources, targets = refs[:jobs], refs[jobs : 2 * jobs]
    held, sems = refs[2 * jobs : 3 * jobs], refs[3 * jobs :]
    barrier = pltpu.get_barrier_semaphore()
    names = sorted(set(axes))
    peers = 0
    for axis in names:
        me, size = lax.axis_index(axis), sizes[axis]
        for step in range(1, size):
            pl.semaphore_signal(
                barrier,
                inc=1,
                device_id={axis: lax.rem(me + step, size)},
                device_id_type=pl.DeviceIdType.MESH,
            )
        peers += size - 1
    pl.semaphore_wait(barrier, peers)
    remote, own = [], []
    for job, axis in enumerate(axes):
        me, size = lax.axis_index(axis), sizes[axis]
        send, recv, local_sem = sems[3 * job : 3 * job + 3]
        for step in range(1, size):
            peer = lax.rem(me + step, size)
            copy = pltpu.make_async_remote_copy(
                src_ref=sources[job].at[peer],
                dst_ref=targets[job].at[me],
                send_sem=send.at[step],
                recv_sem=recv.at[step],
                device_id={axis: peer},
                device_id_type=pl.DeviceIdType.MESH,
            )
            copy.start()
            arriving = pltpu.make_async_remote_copy(
                src_ref=sources[job].at[peer],
                dst_ref=targets[job].at[lax.rem(me + size - step, size)],
                send_sem=send.at[step],
                recv_sem=recv.at[step],
                device_id={axis: peer},
                device_id_type=pl.DeviceIdType.MESH,
            )
            remote.append((copy, arriving))
        take = pltpu.make_async_copy(sources[job].at[me], held[job], local_sem)
        keep = pltpu.make_async_copy(held[job], targets[job].at[me], local_sem)
        take.start()
        own.append((take, keep))
    for take, keep in own:
        take.wait()
        keep.start()
    for take, keep in own:
        keep.wait()
    for copy, arriving in remote:
        copy.wait_send()
        arriving.wait_recv()


def exchange(arrays, axes, sizes, collective_id):
    scratch = [pltpu.VMEM(a.shape[1:], a.dtype) for a in arrays]
    for axis in axes:
        scratch += [pltpu.SemaphoreType.DMA((sizes[axis],))] * 2 + [pltpu.SemaphoreType.DMA]
    return pl.pallas_call(
        functools.partial(exchange_kernel, axes, sizes),
        out_shape=tuple(jax.ShapeDtypeStruct(a.shape, a.dtype) for a in arrays),
        in_specs=[pl.BlockSpec(memory_space=pl.ANY)] * len(arrays),
        out_specs=tuple(pl.BlockSpec(memory_space=pl.ANY) for _ in arrays),
        scratch_shapes=scratch,
        compiler_params=pltpu.CompilerParams(
            collective_id=collective_id, has_side_effects=True
        ),
        name="exchange",
    )(*arrays)


def edge_masks(cells, side):
    row = lax.broadcasted_iota(jnp.int32, (cells, LANES), 0)
    col = lax.rem(row, side)
    one = lambda keep: keep.astype(jnp.float32)
    return (
        one(row >= side),
        one(row < cells - side),
        one(col >= 1),
        one(col < side - 1),
    )


def row_neighbours(field, masks, side):
    cells = field.shape[0]
    above = pltpu.roll(field, side, 0) * masks[0]
    below = pltpu.roll(field, cells - side, 0) * masks[1]
    return (above, below)


def col_previous(field, masks):
    return pltpu.roll(field, 1, 0) * masks[2]


def col_next(field, masks):
    return pltpu.roll(field, field.shape[0] - 1, 0) * masks[3]


ROWS = 48


def forward_kernel(
    live_ref, owned_ref, back_ref, w_in_ref, kernel_ref, gain_ref,
    pooled_ref, normed_ref, hidden_ref, spatial_ref, squeeze_ref, excite_ref,
):
    columns, batch, cells, narrow = owned_ref.shape
    width = columns * narrow
    side = math.isqrt(cells)
    first = pl.program_id(0) * batch
    gain = gain_ref[...].astype(jnp.float32)
    for b in range(batch):
        keep = live_ref[first + b] > 0
        for r in range(0, cells, ROWS):
            rows = slice(r, r + ROWS)
            pieces = [owned_ref[c, b, rows, :] for c in range(columns)]
            pooled = jnp.concatenate(pieces, axis=-1)
            wide = jnp.where(keep, pooled.astype(jnp.float32), 0.0)
            pooled_ref[b, rows, :] = wide.astype(jnp.bfloat16)
            average = jnp.mean(wide, axis=-1, keepdims=True)
            centred = wide - average
            variance = jnp.mean(centred * centred, axis=-1, keepdims=True)
            standard = centred * lax.rsqrt(variance + NORM_EPS)
            normed_ref[b, rows, :] = (standard * gain).astype(jnp.bfloat16)
    hidden = jnp.dot(
        normed_ref[...].reshape(batch * cells, width),
        w_in_ref[...],
        preferred_element_type=jnp.float32,
    )
    hidden_ref[...] = hidden.reshape(batch, cells, width)
    masks = edge_masks(cells, side)
    for b in range(batch):

        @pl.loop(0, width // LANES)
        def _(part):
            lanes = pl.ds(pl.multiple_of(part * LANES, LANES), LANES)
            value = hidden_ref[b, :, lanes]
            act = value * jax.nn.sigmoid(value)
            above, below = row_neighbours(act, masks, side)
            taps = kernel_ref[:, lanes]
            spread = [
                taps[c : c + 1] * above + taps[3 + c : 4 + c] * act + taps[6 + c : 7 + c] * below
                for c in range(3)
            ]
            spatial = spread[1] + col_previous(spread[0], masks) + col_next(spread[2], masks)
            spatial_ref[b, :, lanes] = spatial
            mixed = spatial * jax.nn.sigmoid(spatial)
            squeeze_ref[b, :, lanes] = jnp.sum(mixed, axis=0, keepdims=True) * (1.0 / cells)
            excite_ref[b, :, lanes] = jnp.sum(
                back_ref[b, :, lanes] * mixed, axis=0, keepdims=True
            )


def forward_call(owned, back_scaled, live, w_in, taps, gain):
    columns, count, cells, narrow = owned.shape
    width = columns * narrow
    batch = 2 if count % 2 == 0 else 1
    block = lambda: pl.BlockSpec((batch, cells, width), lambda g, live: (g, 0, 0))
    row = lambda: pl.BlockSpec((batch, 1, width), lambda g, live: (g, 0, 0))
    whole = lambda a: pl.BlockSpec(a.shape, lambda g, live: (0,) * a.ndim)
    wide = lambda kind: jax.ShapeDtypeStruct((count, cells, width), kind)
    line = jax.ShapeDtypeStruct((count, 1, width), jnp.float32)
    return pl.pallas_call(
        forward_kernel,
        out_shape=(
            wide(jnp.bfloat16), wide(jnp.bfloat16), wide(jnp.float32), wide(jnp.float32), line, line,
        ),
        grid_spec=pltpu.PrefetchScalarGridSpec(
            num_scalar_prefetch=1,
            grid=(count // batch,),
            in_specs=[
                pl.BlockSpec((columns, batch, cells, narrow), lambda g, live: (0, g, 0, 0)),
                block(), whole(w_in), whole(taps), whole(gain),
            ],
            out_specs=[block(), block(), block(), block(), row(), row()],
        ),
        compiler_params=params(),
        cost_estimate=pl.CostEstimate(
            flops=2 * count * cells * width * width,
            bytes_accessed=30 * count * cells * width,
            transcendentals=4 * count * cells * width,
        ),
        name="forward",
    )(live, owned, back_scaled, w_in, taps, gain)


def backward_kernel(
    pooled_ref, hidden_ref, spatial_ref, back_ref, up_ref, excite_ref, shift_ref,
    w_in_t_ref, kernel_ref, gain_ref,
    back_hidden_ref, back_in_ref, taps_ref, gain_grad_ref, normed_ref,
):
    columns, batch, cells, narrow = back_in_ref.shape
    width = columns * narrow
    side = math.isqrt(cells)

    @pl.when(pl.program_id(0) == 0)
    def _():
        taps_ref[...] = jnp.zeros_like(taps_ref)
        gain_grad_ref[...] = jnp.zeros_like(gain_grad_ref)

    masks = edge_masks(cells, side)
    for b in range(batch):

        @pl.loop(0, width // LANES)
        def _(part):
            lanes = pl.ds(pl.multiple_of(part * LANES, LANES), LANES)
            taps = kernel_ref[:, lanes]
            spatial = spatial_ref[b, :, lanes]
            sig = jax.nn.sigmoid(spatial)
            back_mixed = back_ref[b, :, lanes] * excite_ref[b, :, lanes] + shift_ref[b, :, lanes]
            back = back_mixed * (sig * (1.0 + spatial * (1.0 - sig)))
            above, below = row_neighbours(back, masks, side)
            spread = [
                taps[c : c + 1] * below + taps[3 + c : 4 + c] * back + taps[6 + c : 7 + c] * above
                for c in range(3)
            ]
            back_act = spread[1] + col_next(spread[0], masks) + col_previous(spread[2], masks)
            value = hidden_ref[b, :, lanes]
            sig = jax.nn.sigmoid(value)
            back_hidden_ref[b, :, lanes] = (
                back_act * (sig * (1.0 + value * (1.0 - sig)))
            ).astype(jnp.bfloat16)
            act = value * sig
            above, below = row_neighbours(act, masks, side)
            sides = (
                pltpu.roll(back * masks[2], cells - 1, 0),
                back,
                pltpu.roll(back * masks[3], 1, 0),
            )
            for a, field in enumerate((above, act, below)):
                for c in range(3):
                    tap = 3 * a + c
                    taps_ref[tap : tap + 1, lanes] += jnp.sum(
                        sides[c] * field, axis=0, keepdims=True
                    )

    normed_ref[...] = jnp.dot(
        back_hidden_ref[...].reshape(batch * cells, width),
        w_in_t_ref[...],
        preferred_element_type=jnp.float32,
    )
    gain = gain_ref[...].astype(jnp.float32)
    for b in range(batch):
        for r in range(0, cells, ROWS):
            rows = slice(r, r + ROWS)
            wide = pooled_ref[b, rows, :].astype(jnp.float32)
            average = jnp.mean(wide, axis=-1, keepdims=True)
            centred = wide - average
            variance = jnp.mean(centred * centred, axis=-1, keepdims=True)
            inverse = lax.rsqrt(variance + NORM_EPS)
            standard = centred * inverse
            back_normed = normed_ref[b * cells + r : b * cells + r + ROWS, :]
            gain_grad_ref[...] += jnp.sum(back_normed * standard, axis=0, keepdims=True)
            back_x = back_normed * gain
            centre = jnp.mean(back_x, axis=-1, keepdims=True)
            along = jnp.mean(back_x * standard, axis=-1, keepdims=True)
            result = up_ref[b, rows, :].astype(jnp.float32) + inverse * (
                back_x - centre - standard * along
            )
            result = result.astype(jnp.bfloat16)
            for c in range(columns):
                back_in_ref[c, b, rows, :] = result[:, c * narrow : (c + 1) * narrow]


def backward_call(
    pooled, hidden, spatial, back_scaled, upstream, excite, shift, w_in_t, taps, gain, columns
):
    count, cells, width = pooled.shape
    narrow = width // columns
    batch = 2 if count % 2 == 0 else 1
    block = lambda: pl.BlockSpec((batch, cells, width), lambda g: (g, 0, 0))
    row = lambda: pl.BlockSpec((batch, 1, width), lambda g: (g, 0, 0))
    whole = lambda shape: pl.BlockSpec(shape, lambda g: (0,) * len(shape))
    return pl.pallas_call(
        backward_kernel,
        out_shape=(
            jax.ShapeDtypeStruct((count, cells, width), jnp.bfloat16),
            jax.ShapeDtypeStruct((columns, count, cells, narrow), jnp.bfloat16),
            jax.ShapeDtypeStruct((9, width), jnp.float32),
            jax.ShapeDtypeStruct((1, width), jnp.float32),
        ),
        grid=(count // batch,),
        in_specs=[
            block(), block(), block(), block(), block(), row(), row(),
            whole(w_in_t.shape), whole(taps.shape), whole(gain.shape),
        ],
        out_specs=[
            block(),
            pl.BlockSpec((columns, batch, cells, narrow), lambda g: (0, g, 0, 0)),
            whole((9, width)),
            whole((1, width)),
        ],
        scratch_shapes=[pltpu.VMEM((batch * cells, width), jnp.float32)],
        compiler_params=params(),
        cost_estimate=pl.CostEstimate(
            flops=2 * count * cells * width * width,
            bytes_accessed=30 * count * cells * width,
            transcendentals=4 * count * cells * width,
        ),
        name="backward",
    )(pooled, hidden, spatial, back_scaled, upstream, excite, shift, w_in_t, taps, gain)


def silu_slope(value):
    sig = jax.nn.sigmoid(value)
    return sig * (1.0 + value * (1.0 - sig))


def pick_row(table, chosen):
    return jnp.sum(jnp.where(chosen[:, None], table, 0), axis=0, dtype=jnp.int32)


def local(
    tiles,
    w_in,
    w_out,
    se_down,
    se_up,
    kernel,
    gain,
    token_grads,
    tile_counts,
    sample_owner,
    sample_rank,
):
    groups = lax.axis_size("enc")
    columns = lax.axis_size("abs")
    group_id = lax.axis_index("enc")
    column_id = lax.axis_index("abs")
    local_tiles = tiles.shape[0]
    owned_rows = token_grads.shape[0]
    capacity = owned_rows * columns
    cells = token_grads.shape[1]
    start, offset, filled = route_tables(tile_counts, sample_owner, sample_rank)
    sources = jnp.arange(groups, dtype=jnp.int32)
    this_group = sources == group_id
    owner_row = pick_row(sample_owner, this_group)
    start_row = pick_row(start, this_group)
    arriving = sample_owner == group_id
    recv_count = jnp.sum(jnp.where(arriving, tile_counts, 0), axis=1, dtype=jnp.int32)
    recv_offset = jnp.sum(jnp.where(arriving, offset, 0), axis=1, dtype=jnp.int32)
    positions = jnp.arange(capacity, dtype=jnp.int32)
    inside = (positions[:, None] >= recv_offset[None, :]) & (
        positions[:, None] < (recv_offset + recv_count)[None, :]
    )
    gather_rows = jnp.sum(
        jnp.where(inside, sources[None, :] * MOST + positions[:, None] - recv_offset[None, :], 0),
        axis=1,
        dtype=jnp.int32,
    )
    occupied = jnp.any(inside, axis=1).astype(jnp.int32)
    tile_ids = jnp.arange(local_tiles, dtype=jnp.int32)
    member = (
        jnp.sum(
            (start_row[None, :] <= tile_ids[:, None]).astype(jnp.int32), axis=1, dtype=jnp.int32
        )
        - 1
    )
    which = member[:, None] == sources[None, :]
    member_owner = jnp.sum(jnp.where(which, owner_row[None, :], 0), axis=1, dtype=jnp.int32)
    member_start = jnp.sum(jnp.where(which, start_row[None, :], 0), axis=1, dtype=jnp.int32)
    unpack_rows = member_owner * MOST + tile_ids - member_start
    filled_here = jnp.sum(jnp.where(this_group, filled, 0), dtype=jnp.int32)
    live = column_id * owned_rows + jnp.arange(owned_rows, dtype=jnp.int32) < filled_here
    width = token_grads.shape[2]
    narrow = tiles.shape[3]
    devices = groups * columns
    flat = (owned_rows * cells, width)
    upstream = jnp.where(live[:, None, None], token_grads, jnp.zeros_like(token_grads))
    back_scaled = jnp.dot(
        upstream.reshape(flat), w_out.T, preferred_element_type=jnp.float32
    ).reshape(upstream.shape)
    taps = kernel.astype(jnp.float32)
    gain_row = gain.reshape(1, width)

    sends = groups * MOST
    send = pool_and_place(tiles, unpack_rows, sends).reshape(groups, MOST, cells, narrow)
    received = lax.all_to_all(send, "enc", split_axis=0, concat_axis=0, tiled=True)
    compact = pick_rows(received.reshape(groups * MOST, cells, narrow), gather_rows)
    owned = lax.all_to_all(
        compact.reshape(columns, owned_rows, cells, narrow),
        "abs",
        split_axis=0,
        concat_axis=0,
        tiled=True,
    )
    pooled, normed, hidden, spatial, squeeze, back_excite = forward_call(
        owned, back_scaled, live.astype(jnp.int32), w_in, taps, gain_row
    )

    exact = functools.partial(jnp.dot, precision=lax.Precision.HIGHEST)
    squeeze = squeeze.reshape(owned_rows, width)
    down, up = se_down.astype(jnp.float32), se_up.astype(jnp.float32)
    squeeze_pre = exact(squeeze, down)
    squeeze_act = jax.nn.silu(squeeze_pre)
    excite = jax.nn.sigmoid(exact(squeeze_act, up))
    back_pre = back_excite.reshape(owned_rows, width) * excite * (1.0 - excite)
    back_squeeze_pre = exact(back_pre, up.T) * silu_slope(squeeze_pre)
    shift = exact(back_squeeze_pre, down.T) / cells

    back_hidden, back_in, taps_term, gain_term = backward_call(
        pooled, hidden, spatial, back_scaled, upstream,
        excite[:, None, :], shift[:, None, :], w_in.T, taps, gain_row, columns,
    )
    scaled = (jax.nn.silu(spatial) * excite[:, None, :]).astype(jnp.bfloat16)
    output = jnp.dot(scaled.reshape(flat), w_out, preferred_element_type=jnp.float32)
    visual = (pooled.astype(jnp.float32) + output.reshape(pooled.shape)).astype(jnp.bfloat16)

    w_out_term = jnp.dot(
        scaled.reshape(flat).T, upstream.reshape(flat), preferred_element_type=jnp.float32
    )
    w_in_term = jnp.dot(
        normed.reshape(flat).T, back_hidden.reshape(flat), preferred_element_type=jnp.float32
    )
    se_up_term = exact(squeeze_act.T, back_pre)
    se_down_term = exact(squeeze.T, back_squeeze_pre)
    share = width // devices
    small = jnp.concatenate(
        [
            taps_term.reshape(9, devices, share).transpose(1, 0, 2).reshape(devices, 9 * share),
            gain_term.reshape(devices, share),
        ],
        axis=1,
    )
    lines = -(-10 * share // width)
    small = jnp.pad(small, ((0, 0), (0, lines * width - 10 * share)))
    dest = lambda term: term.astype(jnp.bfloat16).reshape(groups, columns, -1, width)
    rest = jnp.concatenate([dest(se_down_term), dest(se_up_term), dest(small)], axis=2)

    sizes = {"enc": groups, "abs": columns}
    back_narrow, *partial = exchange(
        [
            back_in,
            w_in_term.astype(jnp.bfloat16).reshape(groups, -1, width),
            w_out_term.astype(jnp.bfloat16).reshape(groups, -1, width),
            rest,
        ],
        ("abs", "enc", "enc", "enc"),
        sizes,
        1,
    )
    returned = place_rows(
        back_narrow.reshape(capacity, cells, narrow), gather_rows, occupied, sends
    )
    partial = [
        jnp.sum(part.astype(jnp.float32), axis=0)
        .astype(jnp.bfloat16)
        .reshape(columns, -1, width)
        for part in partial
    ]
    arrived, *parts = exchange(
        [returned.reshape(groups, MOST, cells, narrow)] + partial,
        ("enc", "abs", "abs", "abs"),
        sizes,
        2,
    )
    tile_grads = pick_and_spread(
        arrived.reshape(sends, cells, narrow), unpack_rows, tiles.shape[1]
    )
    w_in_sum, w_out_sum, rest_sum = [
        jnp.sum(part.astype(jnp.float32), axis=0) for part in parts
    ]
    down_rows = se_down.size // (devices * width)
    up_rows = se_up.size // (devices * width)
    scale = 1.0 / math.sqrt(groups * local_tiles * cells)
    lasts = rest_sum[down_rows + up_rows :].reshape(-1)
    return (
        visual,
        tile_grads,
        w_in_sum * scale,
        w_out_sum * scale,
        rest_sum[:down_rows].reshape(-1, se_down.shape[1]) * scale,
        rest_sum[down_rows : down_rows + up_rows] * scale,
        lasts[: 9 * share].reshape(9, share) * scale,
        lasts[9 * share : 10 * share] * scale,
    )


def solution(mesh):
    return jax.shard_map(
        local,
        mesh=mesh,
        in_specs=(
            P("enc", None, None, "abs"),
            P(),
            P(),
            P(),
            P(),
            P(),
            P(),
            P(("enc", "abs"), None, None),
            P(),
            P(),
            P(),
        ),
        out_specs=(
            P(("enc", "abs"), None, None),
            P("enc", None, None, "abs"),
            P(("enc", "abs"), None),
            P(("enc", "abs"), None),
            P(("enc", "abs"), None),
            P(("enc", "abs"), None),
            P(None, ("enc", "abs")),
            P(("enc", "abs")),
        ),
        check_vma=False,
    )
```

```python
import functools
import math

import jax
import jax.numpy as jnp
from jax import lax
from jax.experimental import pallas as pl
from jax.experimental.pallas import tpu as pltpu
from jax.sharding import PartitionSpec as P

MOST = 9


NORM_EPS = 1e-06


def route_tables(counts, owners, ranks):
    groups = counts.shape[0]
    start = jnp.cumsum(counts, axis=1, dtype=jnp.int32) - counts
    flat_counts = counts.reshape(-1)
    flat_owners = owners.reshape(-1)
    flat_ranks = ranks.reshape(-1)
    ahead = (flat_owners[:, None] == flat_owners[None, :]) & (
        flat_ranks[None, :] < flat_ranks[:, None]
    )
    offset = jnp.sum(jnp.where(ahead, flat_counts[None, :], 0), axis=1, dtype=jnp.int32).reshape(
        groups, groups
    )
    owner_axis = jnp.arange(groups, dtype=jnp.int32)
    filled = jnp.sum(
        jnp.where(flat_owners[None, :] == owner_axis[:, None], flat_counts[None, :], 0),
        axis=1,
        dtype=jnp.int32,
    )
    return (start, offset, filled)


VMEM_BYTES = 50 * 1024 * 1024
LANES = 128


def params():
    return pltpu.CompilerParams(vmem_limit_bytes=VMEM_BYTES)


def first_cells(cells):
    return (cells // 16 + 1) // 2 * 16


def pool_kernel(rows_ref, tile_ref, out_ref, rest_ref, half_ref):
    grid, channels = tile_ref.shape[1], tile_ref.shape[3]
    side = grid // 2
    wide = tile_ref[0].astype(jnp.float32).reshape(side, 2, grid, channels)
    half = (wide[:, 0] + wide[:, 1]).reshape(side * grid, channels)
    cells = side * side
    for part in range(channels // LANES):
        lanes = slice(part * LANES, (part + 1) * LANES)
        half_ref[part] = half[:, lanes]
        even = half_ref[part, pl.ds(0, cells, stride=2), :]
        odd = half_ref[part, pl.ds(1, cells, stride=2), :]
        pooled = ((even + odd) * 0.25).astype(jnp.bfloat16)
        cut = out_ref.shape[1]
        out_ref[0, :, lanes] = pooled[:cut]
        rest_ref[0, :, lanes] = pooled[cut:]


def pool_and_place(tiles, rows, sends):
    count, grid, _, channels = tiles.shape
    cells = (grid // 2) ** 2
    parts = (first_cells(cells), cells - first_cells(cells))
    return pl.pallas_call(
        pool_kernel,
        out_shape=[
            jax.ShapeDtypeStruct((sends, part, channels), jnp.bfloat16) for part in parts
        ],
        grid_spec=pltpu.PrefetchScalarGridSpec(
            num_scalar_prefetch=1,
            grid=(count,),
            in_specs=[pl.BlockSpec((1, grid, grid, channels), lambda g, rows: (g, 0, 0, 0))],
            out_specs=[
                pl.BlockSpec((1, part, channels), lambda g, rows: (rows[g], 0, 0))
                for part in parts
            ],
            scratch_shapes=[pltpu.VMEM((channels // LANES, 2 * cells, LANES), jnp.float32)],
        ),
        compiler_params=params(),
        name="pool_and_place",
    )(rows, tiles)


def spread_kernel(rows_ref, grads_ref, out_ref, half_ref):
    grid, channels = out_ref.shape[1], out_ref.shape[3]
    side = grid // 2
    cells = side * side
    for part in range(channels // LANES):
        lanes = slice(part * LANES, (part + 1) * LANES)
        quarter = grads_ref[0, :, lanes].astype(jnp.float32) * 0.25
        half_ref[part, pl.ds(0, cells, stride=2), :] = quarter
        half_ref[part, pl.ds(1, cells, stride=2), :] = quarter
        half = half_ref[part].reshape(side, 1, grid, LANES)
        whole = jnp.broadcast_to(half, (side, 2, grid, LANES)).reshape(grid, grid, LANES)
        out_ref[0, :, :, lanes] = whole.astype(jnp.bfloat16)


def pick_and_spread(grads, rows, grid):
    _, cells, channels = grads.shape
    count = rows.shape[0]
    return pl.pallas_call(
        spread_kernel,
        out_shape=jax.ShapeDtypeStruct((count, grid, grid, channels), jnp.bfloat16),
        grid_spec=pltpu.PrefetchScalarGridSpec(
            num_scalar_prefetch=1,
            grid=(count,),
            in_specs=[pl.BlockSpec((1, cells, channels), lambda g, rows: (rows[g], 0, 0))],
            out_specs=pl.BlockSpec((1, grid, grid, channels), lambda g, rows: (g, 0, 0, 0)),
            scratch_shapes=[pltpu.VMEM((channels // LANES, 2 * cells, LANES), jnp.float32)],
        ),
        compiler_params=params(),
        name="pick_and_spread",
    )(rows, grads)


def copy_kernel(rows_ref, source_ref, out_ref, sems):
    count = out_ref.shape[0]

    def one(g):
        return pltpu.make_async_copy(source_ref.at[rows_ref[g]], out_ref.at[g], sems.at[g])

    @pl.loop(0, count)
    def _(g):
        one(g).start()

    @pl.loop(0, count)
    def _(g):
        one(g).wait()


def pick_rows(source, rows):
    count = rows.shape[0]
    return pl.pallas_call(
        copy_kernel,
        out_shape=jax.ShapeDtypeStruct((count,) + source.shape[1:], source.dtype),
        grid_spec=pltpu.PrefetchScalarGridSpec(
            num_scalar_prefetch=1,
            grid=(),
            in_specs=[pl.BlockSpec(memory_space=pl.ANY)],
            out_specs=pl.BlockSpec(memory_space=pltpu.VMEM),
            scratch_shapes=[pltpu.SemaphoreType.DMA((count,))],
        ),
        compiler_params=params(),
        name="pick_rows",
    )(rows, source)


def place_kernel(rows_ref, live_ref, source_ref, out_ref, sems):
    count = source_ref.shape[0]

    def one(g):
        return pltpu.make_async_copy(source_ref.at[g], out_ref.at[rows_ref[g]], sems.at[g])

    @pl.loop(0, count)
    def _(g):
        @pl.when(live_ref[g] > 0)
        def _():
            one(g).start()

    @pl.loop(0, count)
    def _(g):
        @pl.when(live_ref[g] > 0)
        def _():
            one(g).wait()


def place_rows(source, rows, live, sends):
    count = rows.shape[0]
    return pl.pallas_call(
        place_kernel,
        out_shape=jax.ShapeDtypeStruct((sends,) + source.shape[1:], source.dtype),
        grid_spec=pltpu.PrefetchScalarGridSpec(
            num_scalar_prefetch=2,
            grid=(),
            in_specs=[pl.BlockSpec(memory_space=pltpu.VMEM)],
            out_specs=pl.BlockSpec(memory_space=pl.ANY),
            scratch_shapes=[pltpu.SemaphoreType.DMA((count,))],
        ),
        compiler_params=params(),
        name="place_rows",
    )(rows, live, source)


def exchange_kernel(axes, sizes, *refs):
    jobs = len(axes)
    sources, targets = refs[:jobs], refs[jobs : 2 * jobs]
    held, sems = refs[2 * jobs : 3 * jobs], refs[3 * jobs :]
    barrier = pltpu.get_barrier_semaphore()
    names = sorted(set(axes))
    peers = 0
    for axis in names:
        me, size = lax.axis_index(axis), sizes[axis]
        for step in range(1, size):
            pl.semaphore_signal(
                barrier,
                inc=1,
                device_id={axis: lax.rem(me + step, size)},
                device_id_type=pl.DeviceIdType.MESH,
            )
        peers += size - 1
    pl.semaphore_wait(barrier, peers)
    remote, own = [], []
    for job, axis in enumerate(axes):
        me, size = lax.axis_index(axis), sizes[axis]
        send, recv, local_sem = sems[3 * job : 3 * job + 3]
        for step in range(1, size):
            peer = lax.rem(me + step, size)
            copy = pltpu.make_async_remote_copy(
                src_ref=sources[job].at[peer],
                dst_ref=targets[job].at[me],
                send_sem=send.at[step],
                recv_sem=recv.at[step],
                device_id={axis: peer},
                device_id_type=pl.DeviceIdType.MESH,
            )
            copy.start()
            arriving = pltpu.make_async_remote_copy(
                src_ref=sources[job].at[peer],
                dst_ref=targets[job].at[lax.rem(me + size - step, size)],
                send_sem=send.at[step],
                recv_sem=recv.at[step],
                device_id={axis: peer},
                device_id_type=pl.DeviceIdType.MESH,
            )
            remote.append((copy, arriving))
        take = pltpu.make_async_copy(sources[job].at[me], held[job], local_sem)
        keep = pltpu.make_async_copy(held[job], targets[job].at[me], local_sem)
        take.start()
        own.append((take, keep))
    for take, keep in own:
        take.wait()
        keep.start()
    for take, keep in own:
        keep.wait()
    for copy, arriving in remote:
        copy.wait_send()
        arriving.wait_recv()


def exchange(arrays, axes, sizes, collective_id):
    scratch = [pltpu.VMEM(a.shape[1:], a.dtype) for a in arrays]
    for axis in axes:
        scratch += [pltpu.SemaphoreType.DMA((sizes[axis],))] * 2 + [pltpu.SemaphoreType.DMA]
    return pl.pallas_call(
        functools.partial(exchange_kernel, axes, sizes),
        out_shape=tuple(jax.ShapeDtypeStruct(a.shape, a.dtype) for a in arrays),
        in_specs=[pl.BlockSpec(memory_space=pl.ANY)] * len(arrays),
        out_specs=tuple(pl.BlockSpec(memory_space=pl.ANY) for _ in arrays),
        scratch_shapes=scratch,
        compiler_params=pltpu.CompilerParams(
            collective_id=collective_id, has_side_effects=True
        ),
        name="exchange",
    )(*arrays)


def edge_masks(cells, side):
    row = lax.broadcasted_iota(jnp.int32, (cells, LANES), 0)
    col = lax.rem(row, side)
    one = lambda keep: keep.astype(jnp.float32)
    return (
        one(row >= side),
        one(row < cells - side),
        one(col >= 1),
        one(col < side - 1),
    )


def row_neighbours(field, masks, side):
    cells = field.shape[0]
    above = pltpu.roll(field, side, 0) * masks[0]
    below = pltpu.roll(field, cells - side, 0) * masks[1]
    return (above, below)


def col_previous(field, masks):
    return pltpu.roll(field, 1, 0) * masks[2]


def col_next(field, masks):
    return pltpu.roll(field, field.shape[0] - 1, 0) * masks[3]


ROWS = 48


def forward_kernel(
    live_ref, owned_ref, rest_ref, back_ref, w_in_ref, kernel_ref, gain_ref,
    pooled_ref, normed_ref, hidden_ref, spatial_ref, squeeze_ref, excite_ref,
):
    columns, batch, cut, narrow = owned_ref.shape
    cells = cut + rest_ref.shape[2]
    width = columns * narrow
    side = math.isqrt(cells)
    first = pl.program_id(0) * batch
    gain = gain_ref[...].astype(jnp.float32)
    for b in range(batch):
        keep = live_ref[first + b] > 0
        for r in range(0, cells, 16):
            rows = slice(r, r + 16)
            source, at = (owned_ref, r) if r < cut else (rest_ref, r - cut)
            pieces = [source[c, b, at : at + 16, :] for c in range(columns)]
            pooled = jnp.concatenate(pieces, axis=-1)
            wide = jnp.where(keep, pooled.astype(jnp.float32), 0.0)
            pooled_ref[b, rows, :] = wide.astype(jnp.bfloat16)
            average = jnp.mean(wide, axis=-1, keepdims=True)
            centred = wide - average
            variance = jnp.mean(centred * centred, axis=-1, keepdims=True)
            standard = centred * lax.rsqrt(variance + NORM_EPS)
            normed_ref[b, rows, :] = (standard * gain).astype(jnp.bfloat16)
    hidden = jnp.dot(
        normed_ref[...].reshape(batch * cells, width),
        w_in_ref[...],
        preferred_element_type=jnp.float32,
    )
    hidden_ref[...] = hidden.reshape(batch, cells, width)
    masks = edge_masks(cells, side)
    for b in range(batch):

        @pl.loop(0, width // LANES)
        def _(part):
            lanes = pl.ds(pl.multiple_of(part * LANES, LANES), LANES)
            value = hidden_ref[b, :, lanes]
            act = value * jax.nn.sigmoid(value)
            above, below = row_neighbours(act, masks, side)
            taps = kernel_ref[:, lanes]
            spread = [
                taps[c : c + 1] * above + taps[3 + c : 4 + c] * act + taps[6 + c : 7 + c] * below
                for c in range(3)
            ]
            spatial = spread[1] + col_previous(spread[0], masks) + col_next(spread[2], masks)
            spatial_ref[b, :, lanes] = spatial
            mixed = spatial * jax.nn.sigmoid(spatial)
            squeeze_ref[b, :, lanes] = jnp.sum(mixed, axis=0, keepdims=True) * (1.0 / cells)
            excite_ref[b, :, lanes] = jnp.sum(
                back_ref[b, :, lanes] * mixed, axis=0, keepdims=True
            )


def forward_call(owned, rest, back_scaled, live, w_in, taps, gain):
    columns, count, cut, narrow = owned.shape
    cells = cut + rest.shape[2]
    width = columns * narrow
    batch = 2 if count % 2 == 0 else 1
    block = lambda: pl.BlockSpec((batch, cells, width), lambda g, live: (g, 0, 0))
    row = lambda: pl.BlockSpec((batch, 1, width), lambda g, live: (g, 0, 0))
    whole = lambda a: pl.BlockSpec(a.shape, lambda g, live: (0,) * a.ndim)
    wide = lambda kind: jax.ShapeDtypeStruct((count, cells, width), kind)
    line = jax.ShapeDtypeStruct((count, 1, width), jnp.float32)
    return pl.pallas_call(
        forward_kernel,
        out_shape=(
            wide(jnp.bfloat16), wide(jnp.bfloat16), wide(jnp.float32), wide(jnp.float32), line, line,
        ),
        grid_spec=pltpu.PrefetchScalarGridSpec(
            num_scalar_prefetch=1,
            grid=(count // batch,),
            in_specs=[
                pl.BlockSpec((columns, batch, cut, narrow), lambda g, live: (0, g, 0, 0)),
                pl.BlockSpec((columns, batch, cells - cut, narrow), lambda g, live: (0, g, 0, 0)),
                block(), whole(w_in), whole(taps), whole(gain),
            ],
            out_specs=[block(), block(), block(), block(), row(), row()],
        ),
        compiler_params=params(),
        cost_estimate=pl.CostEstimate(
            flops=2 * count * cells * width * width,
            bytes_accessed=30 * count * cells * width,
            transcendentals=4 * count * cells * width,
        ),
        name="forward",
    )(live, owned, rest, back_scaled, w_in, taps, gain)


def backward_kernel(
    pooled_ref, hidden_ref, spatial_ref, back_ref, up_ref, excite_ref, shift_ref,
    w_in_t_ref, kernel_ref, gain_ref,
    back_hidden_ref, back_in_ref, taps_ref, gain_grad_ref, normed_ref,
):
    columns, batch, cells, narrow = back_in_ref.shape
    width = columns * narrow
    side = math.isqrt(cells)

    @pl.when(pl.program_id(0) == 0)
    def _():
        taps_ref[...] = jnp.zeros_like(taps_ref)
        gain_grad_ref[...] = jnp.zeros_like(gain_grad_ref)

    masks = edge_masks(cells, side)
    for b in range(batch):

        @pl.loop(0, width // LANES)
        def _(part):
            lanes = pl.ds(pl.multiple_of(part * LANES, LANES), LANES)
            taps = kernel_ref[:, lanes]
            spatial = spatial_ref[b, :, lanes]
            sig = jax.nn.sigmoid(spatial)
            back_mixed = back_ref[b, :, lanes] * excite_ref[b, :, lanes] + shift_ref[b, :, lanes]
            back = back_mixed * (sig * (1.0 + spatial * (1.0 - sig)))
            above, below = row_neighbours(back, masks, side)
            spread = [
                taps[c : c + 1] * below + taps[3 + c : 4 + c] * back + taps[6 + c : 7 + c] * above
                for c in range(3)
            ]
            back_act = spread[1] + col_next(spread[0], masks) + col_previous(spread[2], masks)
            value = hidden_ref[b, :, lanes]
            sig = jax.nn.sigmoid(value)
            back_hidden_ref[b, :, lanes] = (
                back_act * (sig * (1.0 + value * (1.0 - sig)))
            ).astype(jnp.bfloat16)
            act = value * sig
            above, below = row_neighbours(act, masks, side)
            sides = (
                pltpu.roll(back * masks[2], cells - 1, 0),
                back,
                pltpu.roll(back * masks[3], 1, 0),
            )
            for a, field in enumerate((above, act, below)):
                for c in range(3):
                    tap = 3 * a + c
                    taps_ref[tap : tap + 1, lanes] += jnp.sum(
                        sides[c] * field, axis=0, keepdims=True
                    )

    normed_ref[...] = jnp.dot(
        back_hidden_ref[...].reshape(batch * cells, width),
        w_in_t_ref[...],
        preferred_element_type=jnp.float32,
    )
    gain = gain_ref[...].astype(jnp.float32)
    for b in range(batch):
        for r in range(0, cells, ROWS):
            rows = slice(r, r + ROWS)
            wide = pooled_ref[b, rows, :].astype(jnp.float32)
            average = jnp.mean(wide, axis=-1, keepdims=True)
            centred = wide - average
            variance = jnp.mean(centred * centred, axis=-1, keepdims=True)
            inverse = lax.rsqrt(variance + NORM_EPS)
            standard = centred * inverse
            back_normed = normed_ref[b * cells + r : b * cells + r + ROWS, :]
            gain_grad_ref[...] += jnp.sum(back_normed * standard, axis=0, keepdims=True)
            back_x = back_normed * gain
            centre = jnp.mean(back_x, axis=-1, keepdims=True)
            along = jnp.mean(back_x * standard, axis=-1, keepdims=True)
            result = up_ref[b, rows, :].astype(jnp.float32) + inverse * (
                back_x - centre - standard * along
            )
            result = result.astype(jnp.bfloat16)
            for c in range(columns):
                back_in_ref[c, b, rows, :] = result[:, c * narrow : (c + 1) * narrow]


def backward_call(
    pooled, hidden, spatial, back_scaled, upstream, excite, shift, w_in_t, taps, gain, columns
):
    count, cells, width = pooled.shape
    narrow = width // columns
    batch = 2 if count % 2 == 0 else 1
    block = lambda: pl.BlockSpec((batch, cells, width), lambda g: (g, 0, 0))
    row = lambda: pl.BlockSpec((batch, 1, width), lambda g: (g, 0, 0))
    whole = lambda shape: pl.BlockSpec(shape, lambda g: (0,) * len(shape))
    return pl.pallas_call(
        backward_kernel,
        out_shape=(
            jax.ShapeDtypeStruct((count, cells, width), jnp.bfloat16),
            jax.ShapeDtypeStruct((columns, count, cells, narrow), jnp.bfloat16),
            jax.ShapeDtypeStruct((9, width), jnp.float32),
            jax.ShapeDtypeStruct((1, width), jnp.float32),
        ),
        grid=(count // batch,),
        in_specs=[
            block(), block(), block(), block(), block(), row(), row(),
            whole(w_in_t.shape), whole(taps.shape), whole(gain.shape),
        ],
        out_specs=[
            block(),
            pl.BlockSpec((columns, batch, cells, narrow), lambda g: (0, g, 0, 0)),
            whole((9, width)),
            whole((1, width)),
        ],
        scratch_shapes=[pltpu.VMEM((batch * cells, width), jnp.float32)],
        compiler_params=params(),
        cost_estimate=pl.CostEstimate(
            flops=2 * count * cells * width * width,
            bytes_accessed=30 * count * cells * width,
            transcendentals=4 * count * cells * width,
        ),
        name="backward",
    )(pooled, hidden, spatial, back_scaled, upstream, excite, shift, w_in_t, taps, gain)


def silu_slope(value):
    sig = jax.nn.sigmoid(value)
    return sig * (1.0 + value * (1.0 - sig))


def pick_row(table, chosen):
    return jnp.sum(jnp.where(chosen[:, None], table, 0), axis=0, dtype=jnp.int32)


def local(
    tiles,
    w_in,
    w_out,
    se_down,
    se_up,
    kernel,
    gain,
    token_grads,
    tile_counts,
    sample_owner,
    sample_rank,
):
    groups = lax.axis_size("enc")
    columns = lax.axis_size("abs")
    group_id = lax.axis_index("enc")
    column_id = lax.axis_index("abs")
    local_tiles = tiles.shape[0]
    owned_rows = token_grads.shape[0]
    capacity = owned_rows * columns
    cells = token_grads.shape[1]
    start, offset, filled = route_tables(tile_counts, sample_owner, sample_rank)
    sources = jnp.arange(groups, dtype=jnp.int32)
    this_group = sources == group_id
    owner_row = pick_row(sample_owner, this_group)
    start_row = pick_row(start, this_group)
    arriving = sample_owner == group_id
    recv_count = jnp.sum(jnp.where(arriving, tile_counts, 0), axis=1, dtype=jnp.int32)
    recv_offset = jnp.sum(jnp.where(arriving, offset, 0), axis=1, dtype=jnp.int32)
    positions = jnp.arange(capacity, dtype=jnp.int32)
    inside = (positions[:, None] >= recv_offset[None, :]) & (
        positions[:, None] < (recv_offset + recv_count)[None, :]
    )
    gather_rows = jnp.sum(
        jnp.where(inside, sources[None, :] * MOST + positions[:, None] - recv_offset[None, :], 0),
        axis=1,
        dtype=jnp.int32,
    )
    occupied = jnp.any(inside, axis=1).astype(jnp.int32)
    tile_ids = jnp.arange(local_tiles, dtype=jnp.int32)
    member = (
        jnp.sum(
            (start_row[None, :] <= tile_ids[:, None]).astype(jnp.int32), axis=1, dtype=jnp.int32
        )
        - 1
    )
    which = member[:, None] == sources[None, :]
    member_owner = jnp.sum(jnp.where(which, owner_row[None, :], 0), axis=1, dtype=jnp.int32)
    member_start = jnp.sum(jnp.where(which, start_row[None, :], 0), axis=1, dtype=jnp.int32)
    unpack_rows = member_owner * MOST + tile_ids - member_start
    filled_here = jnp.sum(jnp.where(this_group, filled, 0), dtype=jnp.int32)
    live = column_id * owned_rows + jnp.arange(owned_rows, dtype=jnp.int32) < filled_here
    width = token_grads.shape[2]
    narrow = tiles.shape[3]
    devices = groups * columns
    flat = (owned_rows * cells, width)
    upstream = jnp.where(live[:, None, None], token_grads, jnp.zeros_like(token_grads))
    back_scaled = jnp.dot(
        upstream.reshape(flat), w_out.T, preferred_element_type=jnp.float32
    ).reshape(upstream.shape)
    taps = kernel.astype(jnp.float32)
    gain_row = gain.reshape(1, width)

    sends = groups * MOST
    sizes = {"enc": groups, "abs": columns}
    first, second = [
        part.reshape((groups, MOST) + part.shape[1:])
        for part in pool_and_place(tiles, unpack_rows, sends)
    ]

    def compact(part):
        rows = part.reshape((sends,) + part.shape[2:])
        return pick_rows(rows, gather_rows).reshape((columns, owned_rows) + part.shape[2:])

    received = lax.all_to_all(first, "enc", split_axis=0, concat_axis=0, tiled=True)
    owned, received = exchange([compact(received), second], ("abs", "enc"), sizes, 3)
    rest_owned = lax.all_to_all(
        compact(received), "abs", split_axis=0, concat_axis=0, tiled=True
    )
    pooled, normed, hidden, spatial, squeeze, back_excite = forward_call(
        owned, rest_owned, back_scaled, live.astype(jnp.int32), w_in, taps, gain_row
    )

    exact = functools.partial(jnp.dot, precision=lax.Precision.HIGHEST)
    squeeze = squeeze.reshape(owned_rows, width)
    down, up = se_down.astype(jnp.float32), se_up.astype(jnp.float32)
    squeeze_pre = exact(squeeze, down)
    squeeze_act = jax.nn.silu(squeeze_pre)
    excite = jax.nn.sigmoid(exact(squeeze_act, up))
    back_pre = back_excite.reshape(owned_rows, width) * excite * (1.0 - excite)
    back_squeeze_pre = exact(back_pre, up.T) * silu_slope(squeeze_pre)
    shift = exact(back_squeeze_pre, down.T) / cells

    back_hidden, back_in, taps_term, gain_term = backward_call(
        pooled, hidden, spatial, back_scaled, upstream,
        excite[:, None, :], shift[:, None, :], w_in.T, taps, gain_row, columns,
    )
    scaled = (jax.nn.silu(spatial) * excite[:, None, :]).astype(jnp.bfloat16)
    output = jnp.dot(scaled.reshape(flat), w_out, preferred_element_type=jnp.float32)
    visual = (pooled.astype(jnp.float32) + output.reshape(pooled.shape)).astype(jnp.bfloat16)

    w_out_term = jnp.dot(
        scaled.reshape(flat).T, upstream.reshape(flat), preferred_element_type=jnp.float32
    )
    w_in_term = jnp.dot(
        normed.reshape(flat).T, back_hidden.reshape(flat), preferred_element_type=jnp.float32
    )
    se_up_term = exact(squeeze_act.T, back_pre)
    se_down_term = exact(squeeze.T, back_squeeze_pre)
    share = width // devices
    small = jnp.concatenate(
        [
            taps_term.reshape(9, devices, share).transpose(1, 0, 2).reshape(devices, 9 * share),
            gain_term.reshape(devices, share),
        ],
        axis=1,
    )
    lines = -(-10 * share // width)
    small = jnp.pad(small, ((0, 0), (0, lines * width - 10 * share)))
    dest = lambda term: term.astype(jnp.bfloat16).reshape(groups, columns, -1, width)
    rest = jnp.concatenate([dest(se_down_term), dest(se_up_term), dest(small)], axis=2)

    back_narrow, *partial = exchange(
        [
            back_in,
            w_in_term.astype(jnp.bfloat16).reshape(groups, -1, width),
            w_out_term.astype(jnp.bfloat16).reshape(groups, -1, width),
            rest,
        ],
        ("abs", "enc", "enc", "enc"),
        sizes,
        1,
    )
    returned = place_rows(
        back_narrow.reshape(capacity, cells, narrow), gather_rows, occupied, sends
    )
    partial = [
        jnp.sum(part.astype(jnp.float32), axis=0)
        .astype(jnp.bfloat16)
        .reshape(columns, -1, width)
        for part in partial
    ]
    arrived, *parts = exchange(
        [returned.reshape(groups, MOST, cells, narrow)] + partial,
        ("enc", "abs", "abs", "abs"),
        sizes,
        2,
    )
    tile_grads = pick_and_spread(
        arrived.reshape(sends, cells, narrow), unpack_rows, tiles.shape[1]
    )
    w_in_sum, w_out_sum, rest_sum = [
        jnp.sum(part.astype(jnp.float32), axis=0) for part in parts
    ]
    down_rows = se_down.size // (devices * width)
    up_rows = se_up.size // (devices * width)
    scale = 1.0 / math.sqrt(groups * local_tiles * cells)
    lasts = rest_sum[down_rows + up_rows :].reshape(-1)
    return (
        visual,
        tile_grads,
        w_in_sum * scale,
        w_out_sum * scale,
        rest_sum[:down_rows].reshape(-1, se_down.shape[1]) * scale,
        rest_sum[down_rows : down_rows + up_rows] * scale,
        lasts[: 9 * share].reshape(9, share) * scale,
        lasts[9 * share : 10 * share] * scale,
    )


def solution(mesh):
    return jax.shard_map(
        local,
        mesh=mesh,
        in_specs=(
            P("enc", None, None, "abs"),
            P(),
            P(),
            P(),
            P(),
            P(),
            P(),
            P(("enc", "abs"), None, None),
            P(),
            P(),
            P(),
        ),
        out_specs=(
            P(("enc", "abs"), None, None),
            P("enc", None, None, "abs"),
            P(("enc", "abs"), None),
            P(("enc", "abs"), None),
            P(("enc", "abs"), None),
            P(("enc", "abs"), None),
            P(None, ("enc", "abs")),
            P(("enc", "abs")),
        ),
        check_vma=False,
    )
```
